32 devices in a mesh: grp: 16 (over z, y, x), rep: 2 (over core).
Axes of the slice: x: 2, y: 2, z: 4, core: 2. Of those that a mesh axis runs over, the one named last changes fastest.
Arguments:
- layer_input: bfloat16 [2, 2, 1024, 2048], P('rep', None, 'grp'), may hold values from -6 to 6
- out_grad: bfloat16 [2, 2, 1024, 2048], P('rep', None, 'grp'), may hold values from -6 to 6
- routes: int32 [2, 2, 1024, 8], P('rep', None, 'grp'), may hold values from 0 to 15, all different within a row; in each aligned block of 64 rows (0 to 63, 64 to 127, ..., all dimensions but the last counted through in order) at most 36 rows name the same one
- norm_in: bfloat16 [2048], P('grp'), may hold values from 0.5 to 1.5
- query_weight: bfloat16 [2048, 4096], P('grp'), may hold values from -0.125 to 0.125
- key_weight: bfloat16 [2048, 512], P('grp'), may hold values from -0.125 to 0.125
- value_weight: bfloat16 [2048, 512], P('grp'), may hold values from -0.125 to 0.125
- query_gain: bfloat16 [128], P('grp'), may hold values from 0.5 to 1.5
- key_gain: bfloat16 [128], P('grp'), may hold values from 0.5 to 1.5
- out_weight: bfloat16 [4096, 2048], P('grp'), may hold values from -0.75 to 0.75
- norm_mid: bfloat16 [2048], P('grp'), may hold values from 0.5 to 1.5
- router: bfloat16 [2048, 16], P('grp'), may hold values from -0.25 to 0.25
- expert_gate: bfloat16 [16, 2048, 768], P('grp'), may hold values from -0.125 to 0.125
- expert_up: bfloat16 [16, 2048, 768], P('grp'), may hold values from -0.125 to 0.125
- expert_down: bfloat16 [16, 768, 2048], P('grp'), may hold values from -0.21875 to 0.21875
Outputs:
- layer_out: bfloat16 [2, 2, 1024, 2048], P('rep', None, 'grp')
- input_grad: float32 [2, 2, 1024, 2048], P('rep', None, 'grp')
- norm_in_grad: float32 [2048], P('grp')
- query_weight_grad: float32 [2048, 4096], P('grp')
- key_weight_grad: float32 [2048, 512], P('grp')
- value_weight_grad: float32 [2048, 512], P('grp')
- query_gain_grad: float32 [128], P('grp')
- key_gain_grad: float32 [128], P('grp')
- out_weight_grad: float32 [4096, 2048], P('grp')
- norm_mid_grad: float32 [2048], P('grp')
- router_grad: float32 [2048, 16], P('grp')
- expert_gate_grad: float32 [16, 2048, 768], P('grp')
- expert_up_grad: float32 [16, 2048, 768], P('grp')
- expert_down_grad: float32 [16, 768, 2048], P('grp')
The draws below stay inside these ranges and needn't reach their ends.
Inputs may be any that keep to these rules, and one draw needn't show every extreme that they name: `routes`: each row names 8 different experts; in each aligned block of 64 rows (the rows of one device in one micro-batch) no expert is named more than 36 times.
All inputs are finite; a program needn't handle non-finite values.
Results may differ from the reference program's by a relative error of at most 0.022.
Values may be sent and summed in bfloat16 or wider, within the bound.
No kernel may reach another device: no remote copies, remote signals or barrier semaphores. Data moves between devices by JAX's collectives and lax.ppermute only.
A program may use at most 384 MiB of HBM per device.

```python
import math
from functools import partial
import jax
import jax.numpy as jnp
import numpy as np
from jax import lax

D = 2048
HEADS = 32
KVH = 4
HD = 128
FF = 768
TOPK = 8
MICRO = 2
BLOCK = 256
TOK_DEV = 64
EXPERTS = 16
QW = 4096
KW = 512
GROUP_TOK = 1024
LENGTH = 1024
REPLICAS = 2
CAP = 36
N_GRP = 16


def raised(drawn, rng, source, target, shards_of, factor):
    def block_of(position):
        return (jnp.arange(drawn.shape[position]) // (drawn.shape[position] // shards_of)).reshape((-1,) + (1,) * (drawn.ndim - 1 - position))

    near = jax.random.permutation(rng, shards_of)[block_of(target)]
    other_side = (block_of(target) + shards_of // 2) % shards_of
    return jnp.where((block_of(source) == near) | (block_of(source) == other_side), factor * drawn, drawn)


def level_of(key, dims, shards, smallest, top_value):
    loudness, own = 1.0, jax.random.fold_in(key, 6)
    for position, parts in shards:
        draws = jnp.exp(jax.random.uniform(jax.random.fold_in(own, position), (parts,), jnp.float32, smallest / len(shards), top_value / len(shards)))
        loudness = loudness * jnp.repeat(draws, dims[position] // parts).reshape([-1 if axis == position else 1 for axis in range(len(dims))])
    return loudness


def assign_block(rng, own, number, rows, number_of, top, reach, slope):
    ranking = jax.random.permutation(rng, number_of)
    packed, usual = shares(number_of, rows * top, reach, slope, True), shares(number_of, rows * top, reach, slope, False)
    places = jnp.arange(number_of)

    def named(sizes, offset_by):
        used = int((sizes > 0).sum())
        fixed = max(1, used // 4)
        shifted = fixed + (places - fixed + offset_by * (used - fixed)) % max(1, number_of - fixed)
        return jnp.zeros((number_of,), jnp.int32).at[ranking[jnp.where(places < fixed, places, shifted)]].set(jnp.asarray(sizes, jnp.int32))

    sizes = jnp.where(number % 4 == 0, named(packed, number // 4), named(usual, number - number // 4 - 1))
    mixed = jax.random.permutation(jax.random.fold_in(own, 3), number_of)
    donor, sink = mixed[0:number_of // 2 * 2:2], mixed[1:number_of // 2 * 2:2]
    slack = jnp.minimum(sizes[donor] - 1, reach - sizes[sink]) // 2
    slack = jnp.where((donor == ranking[0]) | (sink == ranking[0]) | (sizes[sink] == 0), 0, jnp.maximum(slack, 0))
    shifted = jax.random.randint(jax.random.fold_in(own, 4), (number_of // 2,), 0, 1 << 20) % (slack + 1)
    sizes = sizes.at[donor].add(-shifted).at[sink].add(shifted)
    labels = jnp.searchsorted(jnp.cumsum(sizes), jnp.arange(rows * top), side="right").astype(jnp.int32)
    grid = labels.reshape(top, rows).T
    grid = grid[jax.random.permutation(jax.random.fold_in(own, 1), rows)]
    offset_by = jax.random.randint(jax.random.fold_in(own, 2), (rows, 1), 0, top)
    return jnp.take_along_axis(grid, (jnp.arange(top)[None, :] + offset_by) % top, axis=1)


def shares(number_of, total, reach, lean, full):
    portions = [(1 << 20) // math.isqrt(grade ** lean) + 1 for grade in range(1, number_of + 1)]
    largest = reach if full else min(reach, max(-(-total // number_of), total * portions[0] // sum(portions)))
    least = 1 if total - largest >= number_of - 1 else 0
    holding, surplus = [largest] + [least] * (number_of - 1), total - largest - least * (number_of - 1)
    while surplus > 0:
        movable = [i for i in range(1, number_of) if holding[i] < largest] or [i for i in range(1, number_of) if holding[i] < reach]
        pool, left = sum([portions[i] for i in movable]), surplus
        for i in movable:
            more = min(reach - holding[i], max(1, left * portions[i] // pool), surplus)
            holding[i] = holding[i] + more
            surplus = surplus - more
    return np.array(holding)


def centred(own_key, shape, deviation, limit, split=(), kind=jnp.bfloat16):
    array = jax.random.normal(own_key, shape, jnp.float32) * deviation
    if len(split) > 0:
        array = level_of(own_key, shape, split, -0.22, 0.18) * array
    return jnp.clip(array, min=-limit, max=limit).astype(kind)


def noise_with(stream_key, extent, scale, limit, pieces, heavy, kind=jnp.bfloat16):
    drawn = scale * jax.random.normal(stream_key, extent, jnp.float32)
    if pieces:
        drawn = drawn * level_of(stream_key, extent, pieces, -0.22, 0.18)
    return jnp.clip(raised(drawn, jax.random.fold_in(stream_key, 3), *heavy), -limit, limit).astype(kind)


def setup_inputs(seed: int = 0) -> dict:
    key_list = jax.random.split(jax.random.key(seed), 16)
    layer_input = noise_with(key_list[0], (REPLICAS, MICRO, GROUP_TOK, D), 1.0, 6.0, ((0, 2), (2, 16)), (2, 3, 16, 2.0))
    out_grad = noise_with(key_list[1], (REPLICAS, MICRO, GROUP_TOK, D), 1.0, 6.0, ((0, 2), (2, 16)), (2, 3, 16, 2.0))
    routes_keys = jax.random.split(jax.random.fold_in(key_list[2], 1), REPLICAS * MICRO * GROUP_TOK // TOK_DEV)
    routes_turns = jax.random.permutation(jax.random.fold_in(key_list[2], 3), REPLICAS * MICRO * GROUP_TOK // TOK_DEV)
    routes = jax.vmap(lambda own, number: assign_block(jax.random.fold_in(key_list[2], 2), own, number, TOK_DEV, EXPERTS, TOPK, CAP, 1))(routes_keys, routes_turns).reshape((REPLICAS, MICRO, GROUP_TOK, TOPK))
    norm_in = jnp.clip(1.0 + 0.1 * jax.random.normal(key_list[3], (D,), jnp.float32), 0.5, 1.5).astype(jnp.bfloat16)
    query_weight = centred(key_list[4], (D, QW), D ** -0.5, 0.125, ((0, 16),))
    key_weight = centred(key_list[5], (D, KW), D ** -0.5, 0.125, ((0, 16),))
    value_weight = centred(key_list[6], (D, KW), D ** -0.5, 0.125, ((0, 16),))
    query_gain = jnp.clip(1.0 + 0.1 * jax.random.normal(key_list[7], (HD,), jnp.float32), 0.5, 1.5).astype(jnp.bfloat16)
    key_gain = jnp.clip(1.0 + 0.1 * jax.random.normal(key_list[8], (HD,), jnp.float32), 0.5, 1.5).astype(jnp.bfloat16)
    out_weight = centred(key_list[9], (QW, D), (QW // 64) ** -0.5, 0.75, ((0, 16),))
    norm_mid = jnp.clip(1.0 + 0.1 * jax.random.normal(key_list[10], (D,), jnp.float32), 0.5, 1.5).astype(jnp.bfloat16)
    router = centred(key_list[11], (D, EXPERTS), (D // 4) ** -0.5, 0.25, ((0, 16),))
    expert_gate = centred(key_list[12], (EXPERTS, D, FF), D ** -0.5, 0.125, ((0, 16),))
    expert_up = centred(key_list[13], (EXPERTS, D, FF), D ** -0.5, 0.125, ((0, 16),))
    expert_down = centred(key_list[14], (EXPERTS, FF, D), FF ** -0.5, 0.21875, ((0, 16),))
    return {"layer_input": layer_input, "out_grad": out_grad, "routes": routes, "norm_in": norm_in, "query_weight": query_weight, "key_weight": key_weight, "value_weight": value_weight, "query_gain": query_gain, "key_gain": key_gain, "out_weight": out_weight, "norm_mid": norm_mid, "router": router, "expert_gate": expert_gate, "expert_up": expert_up, "expert_down": expert_down}


EPS = 1e-06
THETA = 1000000.0
NEGATIVE = -1e+30
HIGH = lax.Precision.HIGHEST

@jax.custom_vjp
def low(v):
    return lax.optimization_barrier(v.astype(jnp.bfloat16)).astype(jnp.float32)

@jax.custom_vjp
def low_back(v):
    return v

def low_keep(v):
    return (low(v), None)

def low_pass(kept, grad):
    return (grad,)

def back_keep(v):
    return (v, None)

def back_low(kept, grad):
    return (low(grad),)
low.defvjp(low_keep, low_pass)
low_back.defvjp(back_keep, back_low)

def norm_rows(values, gain):
    return values * lax.rsqrt(lax.optimization_barrier(jnp.mean(values * values, axis=-1, keepdims=True)) + EPS) * gain

def rotate(values, cosine, sine):
    half_size = values.shape[-1] // 2
    first = values[..., :half_size]
    second = values[..., half_size:]
    return jnp.concatenate([first * cosine - second * sine, second * cosine + first * sine], axis=-1)

def rope_tables():
    half_size = HD // 2
    inverse = THETA ** (-(jnp.arange(half_size, dtype=jnp.float32) * 2.0 / HD))
    angle = jnp.arange(LENGTH, dtype=jnp.float32)[:, None] * inverse[None, :]
    return (jnp.cos(angle), jnp.sin(angle))

def attend(weights, sequence):
    norm_in, query_weight, key_weight, value_weight, query_gain, key_gain, out_weight = weights[:7]
    cosine, sine = rope_tables()
    blocks = jnp.arange(LENGTH, dtype=jnp.int32) // BLOCK
    visible = blocks[None, :] <= blocks[:, None]
    low_in = low(norm_rows(sequence, norm_in))
    query_pre = low_back(jnp.dot(low_in, query_weight, precision=HIGH)).reshape(LENGTH, KVH, HEADS // KVH, HD)
    key_pre = low_back(jnp.dot(low_in, key_weight, precision=HIGH)).reshape(LENGTH, KVH, HD)
    values = low_back(low(jnp.dot(low_in, value_weight, precision=HIGH))).reshape(LENGTH, KVH, HD)
    queries = low(rotate(norm_rows(query_pre, query_gain), cosine[:, None, None, :], sine[:, None, None, :]))
    keys = low(rotate(norm_rows(key_pre, key_gain), cosine[:, None, :], sine[:, None, :]))
    scores = low_back(jnp.einsum('qkgd,nkd->kgqn', queries, keys, precision=HIGH) * (1.0 / math.sqrt(HD)))
    scores = jnp.where(visible, scores, NEGATIVE)
    probs = low(jax.nn.softmax(scores, axis=-1))
    attended = low_back(low(jnp.einsum('kgqn,nkd->qkgd', probs, values, precision=HIGH))).reshape(LENGTH, HEADS * HD)
    return sequence + low_back(jnp.dot(attended, out_weight, precision=HIGH))

def expert_apply(operands):
    rows_in, gate_w, up_w, down_w = operands
    gate_pre = low_back(jnp.dot(rows_in, gate_w, precision=HIGH))
    up_pre = low_back(jnp.dot(rows_in, up_w, precision=HIGH))
    hidden = low(jax.nn.silu(gate_pre) * up_pre)
    return low_back(low(jnp.dot(hidden, down_w, precision=HIGH)))

def batch_forward(weights, batch):
    tokens_in, chosen, target, source = batch
    norm_mid, router, expert_gate, expert_up, expert_down = weights[7:]
    mid = lax.map(jax.checkpoint(partial(attend, weights)), tokens_in.reshape(-1, LENGTH, D)).reshape(-1, D)
    low_mid = low(norm_rows(mid, norm_mid))
    logits = low_back(jnp.dot(low_mid, router, precision=HIGH))
    picks = (chosen[:, :, None] == jnp.arange(EXPERTS, dtype=jnp.int32)[None, None, :]).astype(jnp.float32)
    gates = jax.nn.softmax(lax.optimization_barrier(jnp.sum(picks * logits[:, None, :], axis=-1)), axis=-1)
    copies = low_back(jnp.broadcast_to(low_mid[:, None, :], (low_mid.shape[0], TOPK, D))).reshape(-1, D)
    padded = jnp.concatenate([copies, jnp.zeros((1, D), jnp.float32)], axis=0)
    buffer = padded[source].reshape(EXPERTS, N_GRP * CAP, D)
    produced = lax.map(jax.checkpoint(expert_apply), (buffer, expert_gate, expert_up, expert_down)).reshape(-1, D)
    slot_out = produced[target].reshape(-1, TOPK, D)
    return mid + lax.optimization_barrier(jnp.sum(gates[:, :, None] * slot_out, axis=1))

def slot_tables(routes):
    blocks = routes.reshape(REPLICAS * MICRO, N_GRP, TOK_DEV * TOPK)
    marks = (blocks[..., None] == jnp.arange(EXPERTS, dtype=jnp.int32)).astype(jnp.int32)
    slots = lax.optimization_barrier(jnp.sum((jnp.cumsum(marks, axis=2) - marks) * marks, axis=3)).astype(jnp.int32)
    owner = jnp.arange(N_GRP, dtype=jnp.int32)[None, :, None]
    target = (blocks * (N_GRP * CAP) + owner * CAP + slots).astype(jnp.int32).reshape(REPLICAS * MICRO, GROUP_TOK * TOPK)
    entries = GROUP_TOK * TOPK

    def invert(target_row):
        return jnp.full((EXPERTS * N_GRP * CAP,), entries, jnp.int32).at[target_row].set(jnp.arange(entries, dtype=jnp.int32))
    return (target, jax.vmap(invert)(target))

def reference(layer_input, out_grad, routes, norm_in, query_weight, key_weight, value_weight, query_gain, key_gain, out_weight, norm_mid, router, expert_gate, expert_up, expert_down):
    target, source = slot_tables(routes)
    chosen = routes.reshape(REPLICAS * MICRO, GROUP_TOK, TOPK)

    def forward(inputs, *weights):
        batches = inputs.reshape(REPLICAS * MICRO, GROUP_TOK, D)
        result = lax.map(jax.checkpoint(partial(batch_forward, weights)), (batches, chosen, target, source))
        return result.reshape(inputs.shape)
    floats = [array_in.astype(jnp.float32) for array_in in (layer_input, norm_in, query_weight, key_weight, value_weight, query_gain, key_gain, out_weight, norm_mid, router, expert_gate, expert_up, expert_down)]
    result, pull = jax.vjp(forward, *floats)
    grads = pull(out_grad.astype(jnp.float32))
    return (result.astype(jnp.bfloat16), grads[0], grads[1], grads[2], grads[3], grads[4], grads[5], grads[6], grads[7], grads[8], grads[9], grads[10], grads[11], grads[12])
```

```python
import math

import jax
import jax.numpy as jnp
from jax import lax
from jax.sharding import PartitionSpec as P

BLOCK = 256
SEQ = 1024
EPS = 1e-06
THETA = 1000000.0
NEGATIVE = -1e30
AXES = ("grp", "rep")
LINES = 4
F32 = jnp.float32
BF16 = jnp.bfloat16


def row_scale(values):
    return lax.rsqrt(jnp.mean(values * values, axis=-1, keepdims=True) + EPS)


def norm_back(grad, values, factor, gain):
    inner = grad * gain
    back = factor * inner - values * factor**3 * jnp.mean(inner * values, axis=-1, keepdims=True)
    return (back, grad * values * factor)


def rotate(values, cosine, sine):
    half = values.shape[-1] // 2
    first, second = values[..., :half], values[..., half:]
    return jnp.concatenate([first * cosine - second * sine, second * cosine + first * sine], axis=-1)


def dot(left, right):
    return lax.dot_general(left, right, (((1,), (0,)), ((), ())), preferred_element_type=F32)


def dot_out(left, right):
    return lax.dot_general(left, right, (((1,), (1,)), ((), ())), preferred_element_type=F32)


def dot_rows(left, right):
    return lax.dot_general(left, right, (((0,), (0,)), ((), ())), preferred_element_type=F32)


def flip_bit(values, axis, bit):
    count = values.shape[axis]
    pieces = [lax.slice_in_dim(values, i, i + bit, axis=axis) for i in range(0, count, bit)]
    order = [i ^ 1 for i in range(len(pieces))]
    return jnp.concatenate([pieces[i] for i in order], axis=axis)


def xor_order(values, axis, mine):
    bit = 1
    while bit < values.shape[axis]:
        values = jnp.where((mine & bit) != 0, flip_bit(values, axis, bit), values)
        bit *= 2
    return values


def build(groups, reps):
    columns = groups // LINES
    sequences = max(1, groups // 16)

    class Moves:
        pass

    def index(g, r):
        return g * reps + r

    def pairs(target):
        return [
            (index(g, r), index(*target(g, r))) for g in range(groups) for r in range(reps)
        ]

    def line(k):
        table = pairs(lambda g, r: (((g // columns) ^ k) * columns + g % columns, r))
        return lambda v: lax.ppermute(v, AXES, table)

    def plane(k):
        table = pairs(lambda g, r: (g ^ k, r))
        return lambda v: lax.ppermute(v, AXES, table)

    def replica(k):
        table = pairs(lambda g, r: (g, r ^ k))
        return lambda v: lax.ppermute(v, AXES, table)

    def home(k):
        def target(g, r):
            sequence, block = g // 16, g % 16
            batch = k ^ (g & 1)
            column = (sequence * 2 + r % 2) * 2 + batch
            return ((block // 4) * columns + column, (r // 2) * 2 + (block // 2) % 2)

        table = pairs(target)
        back = [(b, a) for a, b in table]
        return (
            lambda v: lax.ppermute(v, AXES, table),
            lambda v: lax.ppermute(v, AXES, back),
        )

    moves = Moves()
    moves.columns = columns
    moves.line = [None] + [line(k) for k in range(1, LINES)]
    moves.plane = [None] + [plane(k) for k in range(1, columns)]
    moves.core = replica(1)
    moves.replicas = [replica(2 * k) for k in range(1, reps // 2)]
    moves.home = [home(0), home(1)]
    del sequences
    return moves


def per_device(
    layer_input,
    out_grad,
    routes,
    norm_in,
    query_weight,
    key_weight,
    value_weight,
    query_gain,
    key_gain,
    out_weight,
    norm_mid,
    router,
    expert_gate,
    expert_up,
    expert_down,
):
    groups, reps = lax.axis_size("grp"), lax.axis_size("rep")
    mv = build(groups, reps)
    columns = mv.columns
    g, r = lax.axis_index("grp"), lax.axis_index("rep")
    tz, gc, core = g // columns, g % columns, r % 2
    odd = (g & 1) != 0
    batches, tokens, width = layer_input.shape[1:]
    experts = groups
    piece = width // groups
    head = query_gain.shape[0] * groups
    heads = query_weight.shape[1] // head
    kv_heads = key_weight.shape[1] // head
    local_heads = heads // (2 * kv_heads)
    scale = 1.0 / math.sqrt(head)
    hidden_half = expert_gate.shape[2] // 2
    rows = batches * tokens
    total = 8 * rows

    def bring(values):
        values = jnp.where(odd, values[::-1], values)
        first, second = (mv.home[k][0](values[k]) for k in range(2))
        got = jnp.stack([first, second])
        return jnp.where(odd, got[::-1], got).reshape((rows,) + values.shape[2:])

    def take_back(values):
        values = values.reshape((2, tokens) + values.shape[1:])
        values = jnp.where(odd, values[::-1], values)
        got = jnp.stack([mv.home[k][1](values[k]) for k in range(2)])
        return jnp.where(odd, got[::-1], got)

    def gather_tokens(values):
        parts = [values] + [mv.line[k](values) for k in range(1, LINES)]
        others = [mv.core(part) for part in parts]
        return jnp.concatenate(parts + others, axis=0)

    def scatter_tokens(partial):
        half = total // 2
        both = partial[:half].astype(F32) + mv.core(partial[half:]).astype(F32)
        blocks = both.reshape((LINES, rows) + both.shape[1:])
        low = blocks.astype(BF16)
        result = blocks[0]
        for k in range(1, LINES):
            result = result + mv.line[k](low[k]).astype(F32)
        return result

    def gather_plane(values, last_bit):
        bits = [b for b in (1, 2, 4, 8) if b < columns]
        if last_bit == 1:
            bits = bits[::-1]
        held = {0: values}
        for b in bits:
            for s in list(held):
                held[s | b] = mv.plane[b](held[s])
        return [held[s] for s in range(columns)]

    def scatter_plane(parts, last_bit):
        bits = [b for b in (1, 2, 4, 8) if b < columns]
        if last_bit == 1:
            bits = bits[::-1]
        held = dict(enumerate(parts))
        for b in bits:
            for s in [s for s in held if s & b]:
                got = mv.plane[b](held.pop(s).astype(BF16))
                held[s ^ b] = held[s ^ b].astype(F32) + got.astype(F32)
        result = held[0]
        if mv.replicas:
            low = result.astype(BF16)
            for move in mv.replicas:
                result = result + move(low).astype(F32)
        return result

    gains = jnp.concatenate([query_gain, key_gain])
    packed = jnp.concatenate(
        [
            norm_in[None],
            norm_mid[None],
            router.T,
            jnp.pad(gains, (0, piece - gains.shape[0]))[None],
        ]
    )
    packed = jnp.stack([packed] + [mv.plane[s](packed) for s in range(1, columns)])
    packed = jnp.stack([packed] + [mv.line[k](packed) for k in range(1, LINES)])
    packed = xor_order(xor_order(packed, 0, tz), 1, gc).reshape(groups, experts + 3, piece)
    small = packed[:, : experts + 2].transpose(1, 0, 2).reshape(experts + 2, width)
    gain_in, gain_mid = small[0].astype(F32), small[1].astype(F32)
    router_t = small[2:]
    part = head // groups
    gain_q = packed[:, experts + 2, :part].reshape(head).astype(F32)
    gain_k = packed[:, experts + 2, part : 2 * part].reshape(head).astype(F32)

    inputs_low = bring(layer_input[0])
    grad_low = bring(out_grad[0])
    named = (routes[0][..., None] == jnp.arange(experts, dtype=jnp.int32)).any(axis=2)
    named = bring(named.astype(BF16))
    inputs = inputs_low.astype(F32)
    grad_out = grad_low.astype(F32)

    per_q = query_weight.reshape(piece, kv_heads, local_heads, 2, head)
    own_q = jnp.where(core == 0, per_q[:, :, :, 0], per_q[:, :, :, 1]).reshape(
        piece, kv_heads, local_heads * head
    )
    qkv = jnp.concatenate(
        [
            own_q,
            key_weight.reshape(piece, kv_heads, head),
            value_weight.reshape(piece, kv_heads, head),
        ],
        axis=2,
    ).transpose(1, 0, 2)
    rel = xor_order(qkv, 0, tz)
    rel = jnp.stack([rel[0]] + [mv.line[k](rel[k]) for k in range(1, LINES)])
    qkv = xor_order(rel, 0, tz)
    w_qkv = jnp.stack(gather_plane(qkv, 2), axis=1).reshape(width, -1)

    out_heads = out_weight.shape[0] // head
    if out_heads == 2:
        own_out = jnp.where(core == 0, out_weight[:head], out_weight[head:])
        w_out = jnp.stack(gather_plane(own_out, 2))
        w_out = xor_order(w_out, 0, gc).reshape(local_heads * head, width)
    else:
        w_out = xor_order(jnp.stack(gather_plane(out_weight, 2)), 0, gc)
        w_out = w_out.reshape(local_heads, 2, head, width)
        w_out = jnp.where(core == 0, w_out[:, 0], w_out[:, 1]).reshape(local_heads * head, width)

    def half_of(values, axis):
        low = lax.slice_in_dim(values, 0, hidden_half, axis=axis)
        high = lax.slice_in_dim(values, hidden_half, 2 * hidden_half, axis=axis)
        return jnp.where(core == 0, low, high)

    w_gate = gather_plane(half_of(expert_gate[0], 1), 1)
    w_up = gather_plane(half_of(expert_up[0], 1), 2)
    w_down = gather_plane(half_of(expert_down[0], 0), 1)

    which = jnp.arange(total, dtype=jnp.int32)
    side, block, inner = which // (LINES * rows), which // rows % LINES, which % rows
    block = block ^ tz
    position = (block * 2 + (side ^ core)) * rows + inner
    block = position // BLOCK
    visible = block[None, :] <= block[:, None]
    inverse = THETA ** (-(jnp.arange(head // 2, dtype=F32) * 2.0 / head))
    angle = position.astype(F32)[:, None] * inverse[None, :]
    cosine, sine = jnp.cos(angle), jnp.sin(angle)

    def swap_columns(values):
        pieces = values.reshape(values.shape[0], LINES, columns, piece)
        return xor_order(pieces, 2, gc).reshape(values.shape)

    scale_in = row_scale(inputs)
    low_in = (inputs * scale_in * gain_in).astype(BF16)
    a1 = gather_tokens(swap_columns(low_in))
    pre = dot(a1, w_qkv)
    q_width = local_heads * head
    query_pre = [pre[:, i * head : (i + 1) * head] for i in range(local_heads)]
    key_pre = pre[:, q_width : q_width + head]
    value_low = pre[:, q_width + head :].astype(BF16)
    query_scale = [row_scale(v) for v in query_pre]
    key_scale = row_scale(key_pre)
    query_rot = [
        rotate(v * s * gain_q, cosine, sine).astype(BF16) for v, s in zip(query_pre, query_scale)
    ]
    key_rot = rotate(key_pre * key_scale * gain_k, cosine, sine).astype(BF16)
    attended, probs_low, log_totals = [], [], []
    for i in range(local_heads):
        scores = jnp.where(visible, dot_out(query_rot[i], key_rot) * scale, NEGATIVE)
        peak = jnp.max(scores, axis=-1, keepdims=True)
        expo = jnp.exp(scores - peak)
        mass = jnp.sum(expo, axis=-1, keepdims=True)
        log_totals.append(peak + jnp.log(mass))
        low = (expo / mass).astype(BF16)
        probs_low.append(low)
        attended.append(dot(low, value_low).astype(BF16))
    attended = jnp.concatenate(attended, axis=1)
    mid = inputs + scatter_tokens(dot(attended, w_out).astype(BF16))
    scale_mid = row_scale(mid)
    low_mid = (mid * scale_mid * gain_mid).astype(BF16)

    a2 = gather_tokens(low_mid)
    dy = gather_tokens(grad_low)
    named_all = gather_tokens(named)

    def gates_of(rows_low, mask):
        logits = jnp.where(mask > 0, dot_out(rows_low, router_t), NEGATIVE)
        return jax.nn.softmax(logits, axis=-1)

    gates_own = gates_of(low_mid, named)
    gates_all = gates_of(a2, named_all).reshape(total, LINES, columns)
    gates_all = xor_order(gates_all, 2, gc)
    gates_line = jnp.sum(
        jnp.where(jnp.arange(LINES)[None, :, None] == tz, gates_all, 0.0), axis=1
    )
    gate_grads, mixed, gate_lows, up_lows = [], [], [], []
    for s in range(columns):
        weight = gates_line[:, s : s + 1]
        gate_pre = dot(a2, w_gate[s])
        up_pre = dot(a2, w_up[s])
        back = dot_out(dy, w_down[s])
        sigmoid = jax.nn.sigmoid(gate_pre)
        silu = gate_pre * sigmoid
        hidden = silu * up_pre
        gate_grads.append(jnp.sum(hidden * back, axis=1))
        mixed.append((hidden * weight).astype(BF16))
        hidden_grad = back * weight
        gate_lows.append(
            (hidden_grad * up_pre * sigmoid * (1.0 + gate_pre * (1.0 - sigmoid))).astype(BF16)
        )
        up_lows.append((hidden_grad * silu).astype(BF16))
    rows_back = sum(
        dot_out(gate_lows[s], w_gate[s]) + dot_out(up_lows[s], w_up[s]) for s in range(columns)
    )
    expert_part = scatter_tokens(rows_back.astype(BF16))
    made = sum(dot(mixed[s], w_down[s]) for s in range(columns))
    layer_out = (mid + scatter_tokens(made.astype(BF16))).astype(BF16)

    gate_grad = jnp.stack(gate_grads, axis=0).reshape(columns, 2, LINES, rows)
    gate_grad = gate_grad[:, 0] + mv.core(gate_grad[:, 1])
    gate_grad = jnp.stack(
        [gate_grad[:, 0]] + [mv.line[k](gate_grad[:, k]) for k in range(1, LINES)]
    )
    gate_grad = xor_order(xor_order(gate_grad, 0, tz), 1, gc).reshape(experts, rows).T
    pick_grad = gates_own * (gate_grad - jnp.sum(gates_own * gate_grad, axis=-1, keepdims=True))
    logit_low = pick_grad.astype(BF16)
    router_part = dot_rows(logit_low, low_mid)
    normed_mid_grad = expert_part + dot(logit_low, router_t)
    mid_back, mid_gain_part = norm_back(normed_mid_grad, mid, scale_mid, gain_mid)
    mid_grad = mid_back + grad_out

    branch = gather_tokens(mid_grad.astype(BF16))
    out_w_part = dot_rows(attended, branch)
    att_grad = dot_out(branch, w_out).astype(BF16)
    key_grad = jnp.zeros((total, head), F32)
    value_grad = jnp.zeros((total, head), F32)
    query_lows = []
    query_gain_part = jnp.zeros((head,), F32)
    for i in range(local_heads):
        grad_i = att_grad[:, i * head : (i + 1) * head]
        scores = dot_out(query_rot[i], key_rot) * scale
        probs = jnp.where(visible, jnp.exp(scores - log_totals[i]), 0.0)
        prob_grad = dot_out(grad_i, value_low)
        score_low = (
            probs * (prob_grad - jnp.sum(probs * prob_grad, axis=-1, keepdims=True))
        ).astype(BF16)
        query_grad = dot(score_low, key_rot) * scale
        key_grad = key_grad + dot_rows(score_low, query_rot[i]) * scale
        value_grad = value_grad + dot_rows(probs_low[i], grad_i)
        query_back, gain_part = norm_back(
            rotate(query_grad, cosine, -sine), query_pre[i], query_scale[i], gain_q
        )
        query_lows.append(query_back.astype(BF16))
        query_gain_part = query_gain_part + jnp.sum(gain_part, axis=0)
    key_back, key_gain_part = norm_back(rotate(key_grad, cosine, -sine), key_pre, key_scale, gain_k)
    qkv_low = jnp.concatenate(
        query_lows + [key_back.astype(BF16), value_grad.astype(BF16)], axis=1
    )
    normed_grad = swap_columns(scatter_tokens(dot_out(qkv_low, w_qkv).astype(BF16)))
    in_back, in_gain_part = norm_back(normed_grad, inputs, scale_in, gain_in)
    input_grad = mid_grad + in_back

    def whole(values, axis):
        other = mv.core(values)
        return jnp.where(
            core == 0,
            jnp.concatenate([values, other], axis=axis),
            jnp.concatenate([other, values], axis=axis),
        ).astype(F32)

    gate_total = whole(scatter_plane([dot_rows(a2, v) for v in gate_lows], 1).astype(BF16), 1)
    up_total = whole(scatter_plane([dot_rows(a2, v) for v in up_lows], 2).astype(BF16), 1)
    down_total = whole(scatter_plane([dot_rows(v, dy) for v in mixed], 1).astype(BF16), 0)

    out_parts = out_w_part.reshape(local_heads, head, width)
    if out_heads == 2:
        out_parts = xor_order(out_parts, 0, gc)
        out_total = whole(scatter_plane([out_parts[s] for s in range(columns)], 2), 0)
    else:
        zeros = jnp.zeros_like(out_parts)
        spread = jnp.where(
            core == 0, jnp.stack([out_parts, zeros], 1), jnp.stack([zeros, out_parts], 1)
        )
        spread = xor_order(spread.reshape(columns, head, width), 0, gc)
        out_total = scatter_plane([spread[s] for s in range(columns)], 2)
        out_total = out_total + mv.core(out_total)

    w_part = dot_rows(a1, qkv_low).reshape(LINES, columns, piece, -1)
    w_part = scatter_plane([w_part[:, s] for s in range(columns)], 2)
    rel = xor_order(w_part, 0, tz)
    rel_low = rel.astype(BF16)
    rel = jnp.stack([rel[0]] + [mv.line[k](rel_low[k]).astype(F32) for k in range(1, LINES)])
    mine = xor_order(rel, 0, tz)
    other = mv.core(mine)
    low, high = jnp.where(core == 0, mine, other), jnp.where(core == 0, other, mine)
    query_total = jnp.stack(
        [v[..., :q_width].reshape(kv_heads, piece, local_heads, head) for v in (low, high)], axis=3
    )
    query_total = query_total.transpose(1, 0, 2, 3, 4).reshape(piece, heads * head)
    both = low + high
    key_total = both[..., q_width : q_width + head].transpose(1, 0, 2).reshape(piece, -1)
    value_total = both[..., q_width + head :].transpose(1, 0, 2).reshape(piece, -1)

    small_part = jnp.concatenate(
        [
            jnp.sum(in_gain_part, axis=0)[None],
            jnp.sum(mid_gain_part, axis=0)[None],
            router_part,
        ]
    )
    small_part = small_part.reshape(experts + 2, groups, piece).transpose(1, 0, 2)
    gain_parts = jnp.stack(
        [query_gain_part.reshape(groups, part), jnp.sum(key_gain_part, axis=0).reshape(groups, part)],
        axis=1,
    ).reshape(groups, 2 * part)
    gain_parts = jnp.pad(gain_parts, ((0, 0), (0, piece - 2 * part)))[:, None]
    small_part = jnp.concatenate([small_part, gain_parts], axis=1)
    small_part = small_part.reshape(LINES, columns, experts + 3, piece)
    small_part = small_part + mv.core(small_part)
    small_part = xor_order(xor_order(small_part, 0, tz), 1, gc)
    small_part = small_part[0] + sum(mv.line[k](small_part[k]) for k in range(1, LINES))
    small_part = small_part[0] + sum(mv.plane[s](small_part[s]) for s in range(1, columns))
    small_part = small_part + sum(move(small_part) for move in mv.replicas)

    return (
        take_back(layer_out)[None],
        take_back(input_grad)[None],
        small_part[0],
        query_total,
        key_total,
        value_total,
        small_part[experts + 2, :part],
        small_part[experts + 2, part : 2 * part],
        out_total,
        small_part[1],
        small_part[2 : experts + 2].T,
        gate_total[None],
        up_total[None],
        down_total[None],
    )


def solution(mesh):
    tokens = P("rep", None, "grp", None)
    rows = P("grp", None)
    vector = P("grp")
    stacked = P("grp", None, None)
    return jax.shard_map(
        per_device,
        mesh=mesh,
        in_specs=(
            tokens,
            tokens,
            tokens,
            vector,
            rows,
            rows,
            rows,
            vector,
            vector,
            rows,
            vector,
            rows,
            stacked,
            stacked,
            stacked,
        ),
        out_specs=(
            tokens,
            tokens,
            vector,
            rows,
            rows,
            rows,
            vector,
            vector,
            rows,
            vector,
            rows,
            stacked,
            stacked,
            stacked,
        ),
        check_vma=False,
    )
```

```python
import math

import jax
import jax.numpy as jnp
from jax import lax
from jax.sharding import PartitionSpec as P

BLOCK = 256
SEQ = 1024
EPS = 1e-06
THETA = 1000000.0
NEGATIVE = -1e30
AXES = ("grp", "rep")
LINES = 4
LANES = 64
F32 = jnp.float32
BF16 = jnp.bfloat16


def row_scale(values):
    return lax.rsqrt(jnp.mean(values * values, axis=-1, keepdims=True) + EPS)


def norm_back(grad, values, factor, gain):
    inner = grad * gain
    back = factor * inner - values * factor**3 * jnp.mean(inner * values, axis=-1, keepdims=True)
    return (back, grad * values * factor)


def rotate(values, cosine, sine):
    half = values.shape[-1] // 2
    first, second = values[..., :half], values[..., half:]
    return jnp.concatenate([first * cosine - second * sine, second * cosine + first * sine], axis=-1)


def dot(left, right):
    return lax.dot_general(left, right, (((1,), (0,)), ((), ())), preferred_element_type=F32)


def dot_out(left, right):
    return lax.dot_general(left, right, (((1,), (1,)), ((), ())), preferred_element_type=F32)


def dot_rows(left, right):
    return lax.dot_general(left, right, (((0,), (0,)), ((), ())), preferred_element_type=F32)


def flip_bit(values, axis, bit):
    count = values.shape[axis]
    pieces = [lax.slice_in_dim(values, i, i + bit, axis=axis) for i in range(0, count, bit)]
    order = [i ^ 1 for i in range(len(pieces))]
    return jnp.concatenate([pieces[i] for i in order], axis=axis)


def xor_order(values, axis, mine):
    bit = 1
    while bit < values.shape[axis]:
        values = jnp.where((mine & bit) != 0, flip_bit(values, axis, bit), values)
        bit *= 2
    return values


def build(groups, reps):
    columns = groups // LINES

    def mover(target):
        table = [
            (g * reps + r, target(g, r)[0] * reps + target(g, r)[1])
            for g in range(groups)
            for r in range(reps)
        ]
        back = [(b, a) for a, b in table]
        return (
            lambda v: lax.ppermute(v, AXES, table),
            lambda v: lax.ppermute(v, AXES, back),
        )

    def home(k):
        def target(g, r):
            sequence, block = g // 16, g % 16
            column = (sequence * 2 + r % 2) * 2 + (k ^ (g & 1))
            return ((block // 4) * columns + column, (r // 2) * 2 + (block // 2) % 2)

        return mover(target)

    def line(k):
        return mover(lambda g, r: (((g // columns) ^ k) * columns + g % columns, r))[0]

    return dict(
        columns=columns,
        line=[None] + [line(k) for k in range(1, LINES)],
        plane=[None] + [mover(lambda g, r, k=k: (g ^ k, r))[0] for k in range(1, columns)],
        core=mover(lambda g, r: (g, r ^ 1))[0],
        replicas=[mover(lambda g, r, k=k: (g, r ^ (2 * k)))[0] for k in range(1, reps // 2)],
        home=[home(0), home(1)],
    )


def split_tail(values):
    high = lax.reduce_precision(values, 8, 7)
    return jnp.concatenate([high, values - high], axis=1).astype(BF16)


def per_device(
    layer_input,
    out_grad,
    routes,
    norm_in,
    query_weight,
    key_weight,
    value_weight,
    query_gain,
    key_gain,
    out_weight,
    norm_mid,
    router,
    expert_gate,
    expert_up,
    expert_down,
):
    groups, reps = lax.axis_size("grp"), lax.axis_size("rep")
    mv = build(groups, reps)
    columns, line, plane, to_core = mv["columns"], mv["line"], mv["plane"], mv["core"]
    sharing = columns // 2
    g, r = lax.axis_index("grp"), lax.axis_index("rep")
    tz, gc, core = g // columns, g % columns, r % 2
    odd = (g & 1) != 0
    batches, tokens, width = layer_input.shape[1:]
    experts = groups
    piece = width // groups
    head = query_gain.shape[0] * groups
    heads = query_weight.shape[1] // head
    kv_heads = key_weight.shape[1] // head
    local_heads = heads // (2 * kv_heads)
    q_width = local_heads * head
    scale = 1.0 / math.sqrt(head)
    hidden = expert_gate.shape[2] // 2
    rows = batches * tokens
    total = 2 * LINES * rows

    def bring(values):
        values = jnp.where(odd, values[::-1], values)
        got = jnp.stack([mv["home"][k][0](values[k]) for k in range(2)])
        return jnp.where(odd, got[::-1], got).reshape((rows,) + values.shape[2:])

    def take_back(values):
        values = values.reshape((2, tokens) + values.shape[1:])
        values = jnp.where(odd, values[::-1], values)
        got = jnp.stack([mv["home"][k][1](values[k]) for k in range(2)])
        return jnp.where(odd, got[::-1], got)

    def line_parts(values):
        first, second = line[1](values), line[2](values)
        return [values, first, second, line[1](second)]

    def gather_tokens(values):
        half = jnp.concatenate(line_parts(values))
        return jnp.concatenate([half, to_core(half)])

    def gather_shared(values):
        parts = []
        for part in line_parts(values):
            parts += [part] + [plane[2 * u](part) for u in range(1, sharing)]
        half = jnp.concatenate(parts)
        return jnp.concatenate([half, to_core(half)])

    def scatter_line(blocks):
        third = line[1](blocks[3].astype(BF16)).astype(F32)
        second = line[2]((blocks[2] + third).astype(BF16)).astype(F32)
        return blocks[0] + line[1](blocks[1].astype(BF16)).astype(F32) + second

    def scatter_tokens(partial):
        half = total // 2
        both = partial[:half].astype(F32) + to_core(partial[half:]).astype(F32)
        return scatter_line([both[k * rows : (k + 1) * rows] for k in range(LINES)])

    def scatter_shared(partial, tail=False):
        half = partial.shape[0] // 2
        both = partial[:half].astype(F32) + to_core(partial[half:]).astype(F32)
        if tail:
            body, extra = both[:, :width], both[:, width:]
            extra = extra[:, :LANES] + extra[:, LANES:]
            low = jnp.concatenate([body.astype(BF16), split_tail(extra)], axis=1)
        else:
            low = both.astype(BF16)
        blocks = []
        for k in range(LINES):
            at = [low[(k * sharing + u) * rows :][:rows] for u in range(sharing)]
            block = at[0].astype(F32)
            for u in range(1, sharing):
                block = block + plane[2 * u](at[u]).astype(F32)
            blocks.append(block)
        return scatter_line(blocks)

    named = (routes[0][..., None] == jnp.arange(experts, dtype=jnp.int32)).any(axis=2)
    named = jnp.pad(named.astype(BF16), ((0, 0), (0, 0), (0, 2 * LANES - experts)))
    brought = bring(jnp.concatenate([layer_input[0], out_grad[0], named], axis=2))
    inputs = brought[:, :width].astype(F32)
    grad_out = brought[:, width : 2 * width].astype(F32)
    named = brought[:, 2 * width :]

    def to_slots(values):
        pieces = [values[:, i * piece : (i + 1) * piece] for i in range(groups)]
        by_slot = [pieces[t * columns + s] for s in range(columns) for t in range(LINES)]
        whole = jnp.stack(by_slot).reshape(columns, LINES, values.shape[0], piece)
        whole = xor_order(whole, 0, gc)
        return jnp.concatenate([whole[s, t] for s in range(columns) for t in range(LINES)], axis=1)

    def from_slots(values):
        count = LINES * piece
        whole = jnp.stack([values[:, s * count : (s + 1) * count] for s in range(columns)])
        whole = xor_order(whole, 0, gc)
        return jnp.concatenate(
            [
                whole[s, :, t * piece : (t + 1) * piece]
                for t in range(LINES)
                for s in range(columns)
            ],
            axis=1,
        )

    gathered = gather_tokens(to_slots(brought[:, :width]))

    per_q = query_weight.reshape(piece, kv_heads, local_heads, 2, head)
    own_q = jnp.where(core == 0, per_q[:, :, :, 0], per_q[:, :, :, 1]).reshape(
        piece, kv_heads, q_width
    )
    qkv = jnp.concatenate(
        [
            own_q,
            key_weight.reshape(piece, kv_heads, head),
            value_weight.reshape(piece, kv_heads, head),
        ],
        axis=2,
    ).transpose(1, 0, 2)
    rel = xor_order(qkv, 0, tz)
    rel = jnp.stack([rel[0]] + [line[k](rel[k]) for k in range(1, LINES)])
    qkv = xor_order(rel, 0, tz).reshape(LINES * piece, -1)
    w_qkv = jnp.concatenate([qkv] + [plane[s](qkv) for s in range(1, columns)])

    gains = jnp.concatenate([query_gain, key_gain])
    packed = jnp.concatenate(
        [
            norm_in[None],
            norm_mid[None],
            router.T,
            jnp.pad(gains, (0, piece - gains.shape[0]))[None],
        ]
    )[None]
    for bit in (b for b in (1, 2, 4, 8) if b < columns):
        packed = jnp.concatenate([packed, plane[bit](packed)])
    packed = packed[None]
    for bit in (1, 2):
        packed = jnp.concatenate([packed, line[bit](packed)])
    packed = xor_order(xor_order(packed, 0, tz), 1, gc).reshape(groups, experts + 3, piece)
    small = packed[:, : experts + 2].transpose(1, 0, 2).reshape(experts + 2, width)
    gain_in, gain_mid = small[:1].astype(F32), small[1:2].astype(F32)
    router_t = small[2:]
    part = head // groups
    gain_q = packed[:, experts + 2, :part].reshape(head).astype(F32)
    gain_k = packed[:, experts + 2, part : 2 * part].reshape(head).astype(F32)

    out_heads = out_weight.shape[0] // head
    own_out = out_weight
    if out_heads == 2:
        own_out = jnp.where(core == 0, out_weight[:head], out_weight[head:])
    w_out = jnp.stack([own_out] + [plane[s](own_out) for s in range(1, columns)])
    w_out = xor_order(w_out, 0, gc)
    if out_heads == 1:
        w_out = w_out.reshape(local_heads, 2, head, width)
        w_out = jnp.where(core == 0, w_out[:, 0], w_out[:, 1])
    w_out = w_out.reshape(q_width, width)

    def half_of(values, axis):
        low = lax.slice_in_dim(values, 0, hidden, axis=axis)
        high = lax.slice_in_dim(values, hidden, 2 * hidden, axis=axis)
        return jnp.where(core == 0, low, high)

    w_own = jnp.concatenate(
        [half_of(expert_gate[0], 1), half_of(expert_up[0], 1), half_of(expert_down[0], 0).T],
        axis=1,
    )
    w_experts = [w_own, plane[1](w_own)]
    expert_ids = [tz * columns + gc, tz * columns + (gc ^ 1)]

    which = jnp.arange(total, dtype=jnp.int32)
    side, block, inner = which // (LINES * rows), which // rows % LINES, which % rows
    position = ((block ^ tz) * 2 + (side ^ core)) * rows + inner
    block = position // BLOCK
    visible = block[None, :] <= block[:, None]
    inverse = THETA ** (-(jnp.arange(head // 2, dtype=F32) * 2.0 / head))
    angle = position.astype(F32)[:, None] * inverse[None, :]
    cosine, sine = jnp.cos(angle), jnp.sin(angle)

    gathered_f = gathered.astype(F32)
    a1 = (gathered_f * row_scale(gathered_f) * to_slots(gain_in)).astype(BF16)
    pre = dot(a1, w_qkv)
    query_pre = [pre[:, i * head : (i + 1) * head] for i in range(local_heads)]
    key_pre = pre[:, q_width : q_width + head]
    value_low = pre[:, q_width + head :].astype(BF16)
    query_scale = [row_scale(v) for v in query_pre]
    key_scale = row_scale(key_pre)
    query_rot = [
        rotate(v * s * gain_q, cosine, sine).astype(BF16) for v, s in zip(query_pre, query_scale)
    ]
    key_rot = rotate(key_pre * key_scale * gain_k, cosine, sine).astype(BF16)
    attended, probs_low, log_totals = [], [], []
    for i in range(local_heads):
        scores = jnp.where(visible, dot_out(query_rot[i], key_rot) * scale, NEGATIVE)
        peak = jnp.max(scores, axis=-1, keepdims=True)
        expo = jnp.exp(scores - peak)
        mass = jnp.sum(expo, axis=-1, keepdims=True)
        log_totals.append(peak + jnp.log(mass))
        low = (expo / mass).astype(BF16)
        probs_low.append(low)
        attended.append(dot(low, value_low).astype(BF16))
    attended = jnp.concatenate(attended, axis=1)
    mid = inputs + scatter_tokens(dot(attended, w_out).astype(BF16))
    scale_mid = row_scale(mid)
    low_mid = (mid * scale_mid * gain_mid).astype(BF16)

    dyx = gather_shared(brought[:, width:])
    dy, named_all = dyx[:, :width], dyx[:, width : width + experts]
    a2 = gather_shared(low_mid)

    def gates_of(rows_low, mask):
        logits = jnp.where(mask > 0, dot_out(rows_low, router_t), NEGATIVE)
        return jax.nn.softmax(logits, axis=-1)

    gates_own = gates_of(low_mid, named[:, :experts])
    gates_all = gates_of(a2, named_all)
    lanes = jnp.arange(experts, dtype=jnp.int32)[None, :]
    spread = jnp.zeros((a2.shape[0], LANES), F32)
    mixed, pair_lows = [], []
    for w, expert in zip(w_experts, expert_ids):
        weight = jnp.sum(jnp.where(lanes == expert, gates_all, 0.0), axis=1, keepdims=True)
        both = dot(a2, w[:, : 2 * hidden])
        gate_pre, up_pre = both[:, :hidden], both[:, hidden:]
        back = dot(dy, w[:, 2 * hidden :])
        sigmoid = jax.nn.sigmoid(gate_pre)
        silu = gate_pre * sigmoid
        made = silu * up_pre
        gate_grad = jnp.sum(made * back, axis=1, keepdims=True)
        spread = jnp.where(jnp.arange(LANES)[None, :] == expert, gate_grad, spread)
        mixed.append((made * weight).astype(BF16))
        made_grad = back * weight
        pair_lows.append(
            jnp.concatenate(
                [
                    made_grad * up_pre * sigmoid * (1.0 + gate_pre * (1.0 - sigmoid)),
                    made_grad * silu,
                ],
                axis=1,
            ).astype(BF16)
        )
    rows_back = sum(dot_out(p, w[:, : 2 * hidden]) for p, w in zip(pair_lows, w_experts))
    rows_back = jnp.concatenate([rows_back.astype(BF16), split_tail(spread)], axis=1)
    came_back = scatter_shared(rows_back, tail=True)
    rows_out = sum(dot_out(m, w[:, 2 * hidden :]) for m, w in zip(mixed, w_experts))
    layer_out = (mid + scatter_shared(rows_out.astype(BF16))).astype(BF16)

    expert_part = came_back[:, :width]
    gate_grad = came_back[:, width : width + experts] + came_back[:, width + LANES :][:, :experts]
    pick_grad = gates_own * (gate_grad - jnp.sum(gates_own * gate_grad, axis=-1, keepdims=True))
    logit_low = pick_grad.astype(BF16)
    router_part = dot_rows(logit_low, low_mid)
    normed_mid_grad = expert_part + dot(logit_low, router_t)
    mid_back, mid_gain_part = norm_back(normed_mid_grad, mid, scale_mid, gain_mid)
    mid_grad = mid_back + grad_out

    branch = gather_tokens(mid_grad.astype(BF16))
    att_grad = dot_out(branch, w_out).astype(BF16)
    key_grad = jnp.zeros((total, head), F32)
    value_grad = jnp.zeros((total, head), F32)
    query_lows = []
    query_gain_part = jnp.zeros((head,), F32)
    for i in range(local_heads):
        grad_i = att_grad[:, i * head : (i + 1) * head]
        scores = dot_out(query_rot[i], key_rot) * scale
        probs = jnp.where(visible, jnp.exp(scores - log_totals[i]), 0.0)
        prob_grad = dot_out(grad_i, value_low)
        score_low = (
            probs * (prob_grad - jnp.sum(probs * prob_grad, axis=-1, keepdims=True))
        ).astype(BF16)
        query_grad = dot(score_low, key_rot) * scale
        key_grad = key_grad + dot_rows(score_low, query_rot[i]) * scale
        value_grad = value_grad + dot_rows(probs_low[i], grad_i)
        query_back, gain_part = norm_back(
            rotate(query_grad, cosine, -sine), query_pre[i], query_scale[i], gain_q
        )
        query_lows.append(query_back.astype(BF16))
        query_gain_part = query_gain_part + jnp.sum(gain_part, axis=0)
    key_back, key_gain_part = norm_back(rotate(key_grad, cosine, -sine), key_pre, key_scale, gain_k)
    qkv_low = jnp.concatenate(
        query_lows + [key_back.astype(BF16), value_grad.astype(BF16)], axis=1
    )
    normed_grad = from_slots(scatter_tokens(dot_out(qkv_low, w_qkv).astype(BF16)))
    in_back, in_gain_part = norm_back(normed_grad, inputs, row_scale(inputs), gain_in)
    input_grad = mid_grad + in_back

    def over_replicas(values):
        low = values.astype(BF16)
        return values + sum(move(low).astype(F32) for move in mv["replicas"])

    def whole(values, axis):
        other = to_core(values)
        return jnp.where(
            core == 0,
            jnp.concatenate([values, other], axis=axis),
            jnp.concatenate([other, values], axis=axis),
        ).astype(F32)

    def scatter_plane(stacked):
        for bit in [b for b in (8, 4, 2, 1) if b < columns]:
            got = plane[bit](stacked[bit : 2 * bit].astype(BF16))
            stacked = stacked[:bit].astype(F32) + got.astype(F32)
        return over_replicas(stacked[0])

    expert_grads = [
        jnp.concatenate([dot_rows(a2, p), dot_rows(dy, m)], axis=1)
        for p, m in zip(pair_lows, mixed)
    ]
    expert_sum = expert_grads[0] + plane[1](expert_grads[1].astype(BF16)).astype(F32)
    expert_sum = over_replicas(expert_sum).astype(BF16)
    gate_total = whole(expert_sum[:, :hidden], 1)
    up_total = whole(expert_sum[:, hidden : 2 * hidden], 1)
    down_total = whole(expert_sum[:, 2 * hidden :].T, 0)

    out_parts = dot_rows(attended, branch).reshape(local_heads, head, width)
    if out_heads == 2:
        out_total = whole(scatter_plane(xor_order(out_parts, 0, gc)), 0)
    else:
        zeros = jnp.zeros_like(out_parts)
        spaced = jnp.where(
            core == 0, jnp.stack([out_parts, zeros], 1), jnp.stack([zeros, out_parts], 1)
        )
        out_total = scatter_plane(xor_order(spaced.reshape(columns, head, width), 0, gc))
        out_total = out_total + to_core(out_total)

    w_part = scatter_plane(dot_rows(a1, qkv_low).reshape(columns, LINES * piece, -1))
    rel = xor_order(w_part.reshape(LINES, piece, -1), 0, tz)
    rel_low = rel.astype(BF16)
    rel = jnp.stack([rel[0]] + [line[k](rel_low[k]).astype(F32) for k in range(1, LINES)])
    mine = xor_order(rel, 0, tz)
    other = to_core(mine)
    low, high = jnp.where(core == 0, mine, other), jnp.where(core == 0, other, mine)
    query_total = jnp.stack(
        [v[..., :q_width].reshape(kv_heads, piece, local_heads, head) for v in (low, high)], axis=3
    )
    query_total = query_total.transpose(1, 0, 2, 3, 4).reshape(piece, heads * head)
    summed = low + high
    key_total = summed[..., q_width : q_width + head].transpose(1, 0, 2).reshape(piece, -1)
    value_total = summed[..., q_width + head :].transpose(1, 0, 2).reshape(piece, -1)

    small_part = jnp.concatenate(
        [
            jnp.sum(in_gain_part, axis=0)[None],
            jnp.sum(mid_gain_part, axis=0)[None],
            router_part,
        ]
    )
    small_part = small_part.reshape(experts + 2, groups, piece).transpose(1, 0, 2)
    gain_parts = jnp.stack(
        [query_gain_part.reshape(groups, part), jnp.sum(key_gain_part, axis=0).reshape(groups, part)],
        axis=1,
    ).reshape(groups, 2 * part)
    gain_parts = jnp.pad(gain_parts, ((0, 0), (0, piece - 2 * part)))[:, None]
    small_part = jnp.concatenate([small_part, gain_parts], axis=1)
    small_part = small_part.reshape(LINES, columns, experts + 3, piece)
    small_part = xor_order(xor_order(small_part, 0, tz), 1, gc)
    small_part = small_part + to_core(small_part)
    for bit in (2, 1):
        small_part = small_part[:bit] + line[bit](small_part[bit : 2 * bit])
    small_part = small_part[0]
    for bit in [b for b in (8, 4, 2, 1) if b < columns]:
        small_part = small_part[:bit] + plane[bit](small_part[bit : 2 * bit])
    small_part = small_part[0]
    small_part = small_part + sum(move(small_part) for move in mv["replicas"])

    return (
        take_back(layer_out)[None],
        take_back(input_grad)[None],
        small_part[0],
        query_total,
        key_total,
        value_total,
        small_part[experts + 2, :part],
        small_part[experts + 2, part : 2 * part],
        out_total,
        small_part[1],
        small_part[2 : experts + 2].T,
        gate_total[None],
        up_total[None],
        down_total[None],
    )


def solution(mesh):
    tokens = P("rep", None, "grp", None)
    rows = P("grp", None)
    vector = P("grp")
    stacked = P("grp", None, None)
    return jax.shard_map(
        per_device,
        mesh=mesh,
        in_specs=(
            tokens,
            tokens,
            tokens,
            vector,
            rows,
            rows,
            rows,
            vector,
            vector,
            rows,
            vector,
            rows,
            stacked,
            stacked,
            stacked,
        ),
        out_specs=(
            tokens,
            tokens,
            vector,
            rows,
            rows,
            rows,
            vector,
            vector,
            rows,
            vector,
            rows,
            stacked,
            stacked,
            stacked,
        ),
        check_vma=False,
    )
```

```python
import math

import jax
import jax.numpy as jnp
from jax import lax
from jax.sharding import PartitionSpec as P

EPS = 1e-06
THETA = 1000000.0
NEGATIVE = -1e30
AXES = ("grp", "rep")
LINES = 4
TAIL = 128
ROWS = 16
F32 = jnp.float32
BF16 = jnp.bfloat16


def row_scale(values):
    return lax.rsqrt(jnp.mean(values * values, axis=-1, keepdims=True) + EPS)


def norm_back(grad, values, factor, gain):
    inner = grad * gain
    back = factor * inner - values * factor**3 * jnp.mean(inner * values, axis=-1, keepdims=True)
    return (back, grad * values * factor)


def dot(left, right):
    return lax.dot_general(left, right, (((1,), (0,)), ((), ())), preferred_element_type=F32)


def dot_out(left, right):
    return lax.dot_general(left, right, (((1,), (1,)), ((), ())), preferred_element_type=F32)


def dot_rows(left, right):
    return lax.dot_general(left, right, (((0,), (0,)), ((), ())), preferred_element_type=F32)


def flip_bit(values, axis, bit):
    count = values.shape[axis]
    pieces = [lax.slice_in_dim(values, i, i + bit, axis=axis) for i in range(0, count, bit)]
    order = [i ^ 1 for i in range(len(pieces))]
    return jnp.concatenate([pieces[i] for i in order], axis=axis)


def xor_order(values, axis, mine):
    bit = 1
    while bit < values.shape[axis]:
        values = jnp.where((mine & bit) != 0, flip_bit(values, axis, bit), values)
        bit *= 2
    return values


def tie(*values):
    return lax.optimization_barrier(values)


def rows_together(parts):
    near, far, other_near, other_far = parts
    count = far.shape[0]
    own = jnp.concatenate([near, far]).reshape(LINES, 1, count, -1)
    other = jnp.concatenate([other_near, other_far]).reshape(LINES, 1, count, -1)
    return jnp.concatenate([own, other], axis=1).reshape(2 * LINES * count, -1)


def two_sides(values):
    sides = values.reshape(LINES, 2, -1, values.shape[1])
    return [sides[:, i].reshape(-1, values.shape[1]) for i in range(2)]


def slots_of(values, slots, piece, shift):
    pieces = values.reshape(values.shape[0], LINES, slots, piece)
    return xor_order(pieces, 2, shift).transpose(0, 2, 1, 3).reshape(values.shape)


def from_slots_of(values, slots, piece, shift):
    pieces = values.reshape(values.shape[0], slots, LINES, piece).transpose(0, 2, 1, 3)
    return xor_order(pieces, 2, shift).reshape(values.shape)


def turn(values, cosine, sine):
    half = values.shape[-1] // 2
    return values * cosine + jnp.concatenate([values[:, half:], values[:, :half]], axis=1) * sine


def block_mask(total, tz):
    block = jnp.arange(total, dtype=jnp.int32) // (total // LINES) ^ tz
    return block[None, :] <= block[:, None]


def attention_forward(scalars, rows, w_slots, w_out, gain_in, gain_q, gain_k, cosine, sine):
    tz, place, shift = scalars[0], scalars[1], scalars[2]
    slots, width = len(w_slots), rows[1].shape[1]
    depth = width // slots
    head = gain_q.shape[1]
    q_width = w_out.shape[0]
    local_heads = q_width // head
    x = rows_together(rows)
    if (depth // LINES) % 128 == 0:
        x = slots_of(x, slots, depth // LINES, shift)
        gain_in = slots_of(gain_in, slots, depth // LINES, shift)
    x = x.astype(F32)
    a1 = (x * row_scale(x) * gain_in).astype(BF16)
    pre = dot(a1, jnp.concatenate([w[:depth] for w in w_slots]))
    scale = 1.0 / math.sqrt(head)
    visible = block_mask(x.shape[0], tz)
    q = jnp.stack(
        [
            turn(u * row_scale(u) * gain_q, cosine, sine).astype(BF16)
            for u in (pre[:, i * head : (i + 1) * head] for i in range(local_heads))
        ]
    )
    q = xor_order(q, 0, place)
    u = pre[:, q_width : q_width + head]
    k = turn(u * row_scale(u) * gain_k, cosine, sine).astype(BF16)
    v = pre[:, q_width + head :].astype(BF16)
    made, inverse = [], []
    for i in range(local_heads):
        expo = jnp.where(visible, jnp.exp(dot_out(q[i], k) * scale), 0.0)
        factor = 1.0 / jnp.sum(expo, axis=1, keepdims=True)
        inverse.append(factor)
        made.append((dot(expo.astype(BF16), v) * factor).astype(BF16))
    o = jnp.concatenate(made, axis=1)
    mine, theirs = two_sides(dot(o, w_out).astype(BF16))
    return a1, pre, q, k, v, o, jnp.stack(inverse), mine, theirs


def attention_backward(
    scalars, grads, w_slots, w_out, gain_q, gain_k, cosine, sine, pre, q, k, v, o, inverse, rows
):
    tz, place, shift = scalars[0], scalars[1], scalars[2]
    slots, width = len(w_slots), rows[1].shape[1]
    depth = width // slots
    head = gain_q.shape[1]
    q_width = w_out.shape[0]
    local_heads = q_width // head
    scale = 1.0 / math.sqrt(head)
    db = rows_together(grads)
    grad = dot_out(db, w_out).astype(BF16)
    visible = block_mask(db.shape[0], tz)
    dk = jnp.zeros(k.shape, F32)
    dv = jnp.zeros(k.shape, F32)
    dqs = []
    for i in range(local_heads):
        at = slice(i * head, (i + 1) * head)
        g = grad[:, at]
        row = jnp.sum(g.astype(F32) * o[:, at].astype(F32), axis=1, keepdims=True)
        probs = jnp.where(visible, jnp.exp(dot_out(q[i], k) * scale), 0.0) * inverse[i]
        low = (probs * (dot_out(g, v) - row)).astype(BF16)
        dqs.append(dot(low, k) * scale)
        dk = dk + dot_rows(low, q[i])
        dv = dv + dot_rows(probs.astype(BF16), g)
    dqs = xor_order(jnp.stack(dqs), 0, place)
    lows, q_gain = [], 0.0
    for i in range(local_heads):
        values = pre[:, i * head : (i + 1) * head]
        back, part = norm_back(turn(dqs[i], cosine, -sine), values, row_scale(values), gain_q)
        lows.append(back.astype(BF16))
        q_gain = q_gain + jnp.sum(part, axis=0)
    values = pre[:, q_width : q_width + head]
    back, part = norm_back(turn(dk * scale, cosine, -sine), values, row_scale(values), gain_k)
    low = jnp.concatenate(lows + [back.astype(BF16), dv.astype(BF16)], axis=1)
    gains = jnp.stack([q_gain, jnp.sum(part, axis=0)])
    da = dot_out(low, jnp.concatenate([w[:depth] for w in w_slots]))
    x = rows_together(rows).astype(F32)
    if (depth // LINES) % 128 == 0:
        da = from_slots_of(da, slots, depth // LINES, shift)
    norm = jnp.sum(da * x * row_scale(x), axis=0)[None]
    mine, theirs = two_sides(da.astype(BF16))
    return db, low, gains, norm, mine, theirs


def expert_rows(ids, a2, dyx, w_experts, router_t):
    width = a2.shape[1]
    mask, dy = dyx[:, width:], dyx[:, :width]
    logits = jnp.where(mask > 0, dot_out(a2, router_t), NEGATIVE)
    gates = jax.nn.softmax(logits, axis=-1)
    lane = jnp.arange(TAIL, dtype=jnp.int32)[None, :]
    hidden = w_experts[0][0].shape[1] // 3
    spread = jnp.zeros(mask.shape, F32)
    pairs, mixes, rows_back = [], [], 0.0
    for e, pieces in enumerate(w_experts):
        w = jnp.concatenate(pieces)
        weight = jnp.sum(jnp.where(lane == ids[e], gates, 0.0), axis=1, keepdims=True)
        both = dot(a2, w[:, : 2 * hidden])
        gate_pre, up_pre = both[:, :hidden], both[:, hidden:]
        back = dot(dy, w[:, 2 * hidden :])
        sigmoid = jax.nn.sigmoid(gate_pre)
        silu = gate_pre * sigmoid
        made = silu * up_pre
        grad = jnp.sum(made * back, axis=1, keepdims=True)
        high = lax.reduce_precision(grad, 8, 7)
        place = ids[len(w_experts)] + ids[e]
        spread = jnp.where(lane == place, high, spread)
        spread = jnp.where(lane == place + TAIL // 4, grad - high, spread)
        mixes.append((made * weight).astype(BF16))
        made_grad = back * weight
        pair = jnp.concatenate(
            [
                made_grad * up_pre * sigmoid * (1.0 + gate_pre * (1.0 - sigmoid)),
                made_grad * silu,
            ],
            axis=1,
        ).astype(BF16)
        pairs.append(pair)
        rows_back = rows_back + dot_out(pair, w[:, : 2 * hidden])
    rows_back = jnp.concatenate([rows_back.astype(BF16), spread.astype(BF16)], axis=1)
    return jnp.concatenate(pairs, axis=1), jnp.concatenate(mixes, axis=1), rows_back


def expert_outputs(mixed, w_experts):
    hidden = w_experts[0][0].shape[1] // 3
    return [
        sum(
            dot_out(m[:, hidden * e : hidden * (e + 1)], jnp.concatenate(w)[:, 2 * hidden :])
            for e, w in enumerate(w_experts)
        ).astype(BF16)
        for m in mixed
    ]


def expert_weight_grads(pairs, mixes, a2, dyx):
    width = a2[0].shape[1]
    units = pairs[0].shape[1] // 2
    hidden = units // 2
    pair = dot_rows(pairs[0], a2[0]) + dot_rows(pairs[1], a2[1])
    down = dot_rows(mixes[0], dyx[0][:, :width]) + dot_rows(mixes[1], dyx[1][:, :width])
    own = jnp.concatenate([pair[:units], down[:hidden]])
    return own, jnp.concatenate([pair[units:], down[hidden:]]).astype(BF16)


def join_expert_grads(core, own, other):
    hidden = own.shape[0] // 3
    first = core[0] == 0
    low, high = jnp.where(first, own, other), jnp.where(first, other, own)
    low, high = low.astype(F32), high.astype(F32)
    return (
        jnp.concatenate([low[:hidden].T, high[:hidden].T], axis=1),
        jnp.concatenate([low[hidden : 2 * hidden].T, high[hidden : 2 * hidden].T], axis=1),
        jnp.concatenate([low[2 * hidden :], high[2 * hidden :]]),
    )


def join_column_grads(core, own, other, head):
    kv_heads, piece, columns = own.shape
    local_heads = columns // head - 2
    q_width = local_heads * head
    first = core[0] == 0
    low, high = jnp.where(first, own, other), jnp.where(first, other, own)
    q = jnp.stack(
        [v[..., :q_width].reshape(kv_heads, piece, local_heads, head) for v in (low, high)], axis=3
    )
    q = q.transpose(1, 0, 2, 3, 4).reshape(piece, -1)
    both = low + high
    k = both[..., q_width : q_width + head].transpose(1, 0, 2).reshape(piece, -1)
    v = both[..., q_width + head :].transpose(1, 0, 2).reshape(piece, -1)
    return q, k, v


def build(groups, reps):
    columns = groups // LINES

    def mover(target):
        table = [
            (g * reps + r, target(g, r)[0] * reps + target(g, r)[1])
            for g in range(groups)
            for r in range(reps)
        ]
        back = [(b, a) for a, b in table]
        return (
            lambda v: lax.ppermute(v, AXES, table),
            lambda v: lax.ppermute(v, AXES, back),
        )

    def home(k):
        def target(g, r):
            sequence, block = g // 16, g % 16
            column = (sequence * 2 + r % 2) * 2 + (k ^ (g & 1))
            return ((block // 4) * columns + column, (r // 2) * 2 + (block // 2) % 2)

        return mover(target)

    def line(k):
        return mover(lambda g, r: (((g // columns) ^ k) * columns + g % columns, r))[0]

    return dict(
        columns=columns,
        line=[None] + [line(k) for k in range(1, LINES)],
        plane=[None] + [mover(lambda g, r, k=k: (g ^ k, r))[0] for k in range(1, columns)],
        core=mover(lambda g, r: (g, r ^ 1))[0],
        replicas=[mover(lambda g, r, k=k: (g, r ^ (2 * k)))[0] for k in range(1, reps // 2)],
        home=[home(0), home(1)],
    )


def per_device(
    layer_input,
    out_grad,
    routes,
    norm_in,
    query_weight,
    key_weight,
    value_weight,
    query_gain,
    key_gain,
    out_weight,
    norm_mid,
    router,
    expert_gate,
    expert_up,
    expert_down,
):
    groups, reps = lax.axis_size("grp"), lax.axis_size("rep")
    mv = build(groups, reps)
    columns, line, plane, to_core = mv["columns"], mv["line"], mv["plane"], mv["core"]
    sharing = columns // 2
    axes = [b for b in (1, 2, 4, 8) if b < columns]
    g, r = lax.axis_index("grp"), lax.axis_index("rep")
    tz, gc, core = g // columns, g % columns, r % 2
    odd = (g & 1) != 0
    batches, tokens, width = layer_input.shape[1:]
    experts = groups
    piece = width // groups
    head = query_gain.shape[0] * groups
    heads = query_weight.shape[1] // head
    kv_heads = key_weight.shape[1] // head
    local_heads = heads // (2 * kv_heads)
    q_width = local_heads * head
    hidden = expert_gate.shape[2] // 2
    rows = batches * tokens
    total = 2 * LINES * rows
    part = head // groups
    wide = width + TAIL

    def at_line(values, i):
        return values[i * rows : (i + 1) * rows]

    def send_home(values):
        values = values.reshape((2, tokens) + values.shape[1:])
        values = jnp.where(odd, values[::-1], values)
        return [mv["home"][k][1](values[k]) for k in range(2)]

    def at_home(got):
        got = jnp.stack(got)
        return jnp.where(odd, got[::-1], got)[None]

    def to_slots(values):
        if piece % 128 == 0:
            return values
        pieces = [values[:, i * piece : (i + 1) * piece] for i in range(groups)]
        by_slot = [pieces[t * columns + s] for s in range(columns) for t in range(LINES)]
        whole = jnp.stack(by_slot).reshape(columns, LINES, values.shape[0], piece)
        whole = xor_order(whole, 0, gc)
        return jnp.concatenate([whole[s, t] for s in range(columns) for t in range(LINES)], axis=1)

    def from_slots(values):
        if piece % 128 == 0:
            return values
        count = LINES * piece
        whole = jnp.stack([values[:, s * count : (s + 1) * count] for s in range(columns)])
        whole = xor_order(whole, 0, gc)
        return jnp.concatenate(
            [
                whole[s, :, t * piece : (t + 1) * piece]
                for t in range(LINES)
                for s in range(columns)
            ],
            axis=1,
        )

    def over_replicas(values):
        low = values.astype(BF16)
        return values + sum(move(low).astype(F32) for move in mv["replicas"])

    def whole(values, other, axis):
        return jnp.where(
            core == 0,
            jnp.concatenate([values, other], axis=axis),
            jnp.concatenate([other, values], axis=axis),
        ).astype(F32)

    def half_of(values, axis):
        low = lax.slice_in_dim(values, 0, hidden, axis=axis)
        high = lax.slice_in_dim(values, hidden, 2 * hidden, axis=axis)
        return jnp.where(core == 0, low, high)

    named = (routes[0][..., None] == jnp.arange(experts, dtype=jnp.int32)).any(axis=2)
    named = jnp.pad(named.astype(F32), ((0, 0), (0, 0), (0, TAIL - experts)))
    named = tie(named)[0].astype(BF16)
    leaving = jnp.concatenate([layer_input[0], out_grad[0], named], axis=2)
    leaving = jnp.where(odd, leaving[::-1], leaving)
    got = [mv["home"][k][0](leaving[k]) for k in range(2)]
    rel = []
    for h in range(kv_heads):
        sides = [
            jnp.concatenate(
                [
                    query_weight[:, ((h * local_heads + i) * 2 + n) * head :][:, :head]
                    for i in range(local_heads)
                ],
                axis=1,
            )
            for n in range(2)
        ]
        at = slice(h * head, (h + 1) * head)
        rel.append(
            jnp.concatenate(
                [jnp.where(core == 0, *sides), key_weight[:, at], value_weight[:, at]], axis=1
            )
        )
    qkv = jnp.stack(rel)
    rel = xor_order(qkv, 0, tz)
    gains = jnp.concatenate([query_gain, key_gain]).astype(F32)
    packed = jnp.concatenate(
        [
            norm_in.astype(F32)[None],
            norm_mid.astype(F32)[None],
            router.astype(F32).T,
            jnp.pad(gains, (0, piece - gains.shape[0]))[None],
        ]
    )
    strips = -(-packed.shape[0] // ROWS)
    packed = jnp.pad(packed, ((0, strips * ROWS - packed.shape[0]), (0, 0)))
    packed = jnp.concatenate([packed[i * ROWS : (i + 1) * ROWS] for i in range(strips)], axis=1)
    packed = jnp.pad(packed, ((0, 0), (0, qkv.shape[2] - packed.shape[1])))
    packed = tie(packed)[0].astype(BF16)
    rel = [jnp.concatenate([rel[k], packed]) for k in range(LINES)]
    rel_got = [line[k](rel[k]) for k in range(1, LINES)]
    out_heads = out_weight.shape[0] // head
    own_out = out_weight
    if out_heads == 2:
        own_out = jnp.where(core == 0, out_weight[:head], out_weight[head:])
    rel_own, own_out, *moved = tie(rel[0], own_out, *got, *rel_got)
    got, rel_got = moved[:2], moved[2:]

    got = jnp.stack(got)
    brought = jnp.where(odd, got[::-1], got).reshape(rows, -1)
    slotted = to_slots(brought[:, :width])
    first, second = line[1](slotted), line[2](slotted)
    qkv = xor_order(jnp.stack([rel_own] + rel_got), 0, tz)
    qkv = jnp.concatenate(
        [qkv[:, :piece].reshape(LINES * piece, -1), qkv[:, piece:].reshape(LINES * ROWS, -1)]
    )
    w_held = {0: qkv}
    for bit in axes[::-1]:
        w_held[bit] = plane[bit](qkv)
    out_held = jnp.stack([own_out, plane[1](own_out)])
    slotted, first, second, out_held, *moved = tie(
        slotted, first, second, out_held, *[w_held[b] for b in [0] + axes]
    )
    for bit, value in zip([0] + axes, moved):
        w_held[bit] = value

    third = line[1](second)
    near_rows = jnp.concatenate([slotted, first, second])
    others = to_core(near_rows)
    for s in range(1, columns):
        if s not in w_held:
            top = max(b for b in axes if s & b)
            w_held[s] = plane[s ^ top](w_held[top])
    for bit in axes[1:]:
        out_held = jnp.concatenate([out_held, plane[bit](out_held)])
    third, others, near_rows, out_held, *w_slots = tie(
        third, others, near_rows, out_held, *[w_held[s] for s in range(columns)]
    )
    w_out = [out_held[s] for s in range(columns)]

    other_third = to_core(third)
    place = gc
    if out_heads == 1:
        place = gc // 2
        swapped = ((gc & 1) ^ core) != 0
        w_out = [jnp.where(swapped, w_out[i + 1], w_out[i]) for i in range(0, columns, 2)]
    w_out = jnp.concatenate(w_out)
    scalars = jnp.stack([tz, place, gc]).astype(jnp.int32)
    which = jnp.arange(total, dtype=jnp.int32)
    block, side, inner = which // (2 * rows), which // rows % 2, which % rows
    position = ((block ^ tz) * 2 + (side ^ core)) * rows + inner
    inverse = THETA ** (-(jnp.arange(head // 2, dtype=F32) * 2.0 / head))
    angle = position.astype(F32)[:, None] * inverse[None, :]
    cosine, sine = jnp.cos(angle), jnp.sin(angle)
    cosine = jnp.concatenate([cosine, cosine], axis=1)
    sine = jnp.concatenate([-sine, sine], axis=1)
    w_own = jnp.concatenate(
        [half_of(expert_gate[0], 1), half_of(expert_up[0], 1), half_of(expert_down[0], 0).T],
        axis=1,
    )
    packed = tie(*[w[LINES * piece :, : strips * piece].astype(F32) for w in w_slots])
    packed = jnp.stack([w.reshape(LINES, ROWS, -1) for w in packed], axis=1)
    packed = xor_order(packed, 1, gc).reshape(groups, ROWS, strips, piece)
    packed = packed.transpose(0, 2, 1, 3).reshape(groups, strips * ROWS, piece)
    other_third, packed, w_out, cosine, sine, w_own, brought = tie(
        other_third, packed, w_out, cosine, sine, w_own, brought
    )
    row_parts = (near_rows, third, others, other_third)
    small = packed[:, : experts + 2].transpose(1, 0, 2).reshape(experts + 2, width)
    gain_in, gain_mid, router_f = tie(small[:1], small[1:2], small[2:])
    router_t = router_f.astype(BF16)
    gain_q = packed[:, experts + 2, :part].reshape(1, head)
    gain_k = packed[:, experts + 2, part : 2 * part].reshape(1, head)

    cuts = [0] + [width * n // 16 for n in (6, 9, 12, 16)]
    w_near = []

    def next_weights():
        n = len(w_near)
        return plane[1](w_own[cuts[n] : cuts[n + 1]])

    grad_rows = brought[:, width:]
    grad_got = [line[n](grad_rows) for n in range(1, LINES)]
    w_got = next_weights()
    a1, pre, q, k, v, attended, inverse, mine, theirs = attention_forward(
        scalars, row_parts, w_slots, w_out, to_slots(gain_in), gain_q, gain_k, cosine, sine
    )
    mine, theirs, w_got, w_own, *grad_got = tie(mine, theirs, w_got, w_own, *grad_got)
    w_near.append(w_got)

    theirs = to_core(theirs)
    grad_own = jnp.concatenate([grad_rows] + grad_got)
    grad_low, grad_high = grad_own[: 2 * rows], grad_own[2 * rows :]
    mine, theirs, grad_low, grad_high = tie(mine, theirs, grad_low, grad_high)
    both = mine.astype(F32) + theirs.astype(F32)

    first = line[1](at_line(both, 1).astype(BF16))
    third = line[1](at_line(both, 3).astype(BF16))
    grads = [[grad_low], [grad_high]]
    got = [plane[2 * u](grad_low) for u in range(1, sharing)]
    w_got = next_weights()
    both, first, third, w_got, w_own, grad_high, *got = tie(
        both, first, third, w_got, w_own, grad_high, *got
    )
    w_near.append(w_got)
    grads[0] += got

    second = line[2]((at_line(both, 2) + third.astype(F32)).astype(BF16))
    got = [plane[2 * u](grad_high) for u in range(1, sharing)]
    w_got = next_weights()
    both, first, second, w_got, w_own, *got = tie(both, first, second, w_got, w_own, *got)
    w_near.append(w_got)
    grads[1] += got
    inputs = brought[:, :width].astype(F32)
    grad_out = brought[:, width : 2 * width].astype(F32)
    mid = inputs + at_line(both, 0) + first.astype(F32) + second.astype(F32)
    scale_mid = row_scale(mid)
    low_mid = (mid * scale_mid * gain_mid).astype(BF16)

    def across(rows_in):
        return [rows_in] + [plane[2 * u](rows_in) for u in range(1, sharing)]

    def join(blocks):
        return jnp.concatenate(blocks)

    first, second = line[1](low_mid), line[2](low_mid)
    a_own = [across(low_mid)]
    grad_half = join(
        [
            at_line(grads[i // 2][u], i % 2)
            for i in range(LINES)
            for u in range(sharing)
        ]
    )
    w_got = next_weights()
    grad_other = to_core(grad_half)
    low_mid, first, second, w_got, grad_half, grad_other, *got = tie(
        low_mid, first, second, w_got, grad_half, grad_other, *a_own[0][1:]
    )
    w_near.append(w_got)
    a_own = [[low_mid] + got]

    third = line[1](second)
    a_own += [across(first), across(second)]
    a_near = join([v for block in a_own[:1] for v in block])
    other_near = to_core(a_near)
    a_near, other_near, third, *got = tie(
        a_near, other_near, third, *a_own[1], *a_own[2]
    )
    far = across(third)
    a_middle = join(got)
    other_middle = to_core(a_middle)
    a_near, other_near, a_middle, other_middle, *far = tie(
        a_near, other_near, a_middle, other_middle, *far
    )
    a_far = join(far)
    other_far = to_core(a_far)
    a_half = join([a_near, a_middle, a_far])
    a_half, other_far = tie(a_half, other_far)
    a_other = join([other_near, other_middle, other_far])

    ids = jnp.stack(
        [tz * columns + gc, tz * columns + (gc ^ 1), core * (TAIL // 2)]
    ).astype(jnp.int32)
    router_pad = jnp.pad(router_t, ((0, TAIL - experts), (0, 0)))
    w_experts = [[w_own], w_near]
    their_pair, their_mixed, their_back = expert_rows(
        ids, a_other, grad_other, w_experts, router_pad
    )
    their_back, a_half = tie(their_back, a_half)
    their_back = to_core(their_back)
    pair, mixed, back = expert_rows(ids, a_half, grad_half, w_experts, router_pad)
    back, their_back, pair, mixed, their_pair, their_mixed = tie(
        back, their_back, pair, mixed, their_pair, their_mixed
    )
    count = sharing * rows

    def summed(mine, theirs, i, u):
        at = i * count + u * rows
        return mine[at : at + rows].astype(F32) + theirs[at : at + rows].astype(F32)

    def to_share(mine, theirs, i):
        return [plane[2 * u](summed(mine, theirs, i, u).astype(BF16)) for u in range(1, sharing)]

    def shared(mine, theirs, i, got):
        return summed(mine, theirs, i, 0) + sum(v.astype(F32) for v in got)

    got = [to_share(back, their_back, i) for i in (3, 2)]
    own, near = expert_weight_grads(
        (pair, their_pair), (mixed, their_mixed), (a_half, a_other), (grad_half, grad_other)
    )
    back, their_back, own, near, mixed, their_mixed, *moved = tie(
        back, their_back, own, near, mixed, their_mixed, *got[0], *got[1]
    )
    line_blocks = {
        3: shared(back, their_back, 3, moved[: sharing - 1]),
        2: shared(back, their_back, 2, moved[sharing - 1 :]),
    }

    ends = [0] + [hidden * n // 8 for n in (6, 17, 24)]
    near = [near[a:b] for a, b in zip(ends[:-1], ends[1:])]
    third = line[1](line_blocks[3].astype(BF16))
    got = to_share(back, their_back, 1)
    near_got = [plane[1](near[0])]
    made, their_made = expert_outputs((mixed, their_mixed), w_experts)
    near_got[0], near[1], third, their_made, made, back, their_back, *moved = tie(
        near_got[0], near[1], third, their_made, made, back, their_back, *got
    )
    line_blocks[1] = shared(back, their_back, 1, moved)

    second = line[2]((line_blocks[2] + third.astype(F32)).astype(BF16))
    first = line[1](line_blocks[1].astype(BF16))
    their_made = to_core(their_made)
    got = to_share(back, their_back, 0)
    first, second, made, their_made, near[1], back, their_back, *got = tie(
        first, second, made, their_made, near[1], back, their_back, *got
    )
    line_blocks[0] = shared(back, their_back, 0, got)
    came_back = line_blocks[0] + first.astype(F32) + second.astype(F32)

    named = brought[:, 2 * width :]
    logits = jnp.where(named[:, :experts] > 0, dot_out(low_mid, router_t), NEGATIVE)
    gates_own = jax.nn.softmax(logits, axis=-1)
    expert_part = came_back[:, :width]
    gate_grad = sum(came_back[:, width + i * (TAIL // 4) :][:, :experts] for i in range(4))
    pick_grad = gates_own * (gate_grad - jnp.sum(gates_own * gate_grad, axis=-1, keepdims=True))
    logit_low = pick_grad.astype(BF16)
    router_part = dot_rows(logit_low, low_mid)
    normed_mid_grad = expert_part + dot(logit_low, router_t)
    mid_back, mid_gain_part = norm_back(normed_mid_grad, mid, scale_mid, gain_mid)
    mid_grad = mid_back + grad_out

    low_grad = mid_grad.astype(BF16)
    first, second = line[1](low_grad), line[2](low_grad)
    got = [to_share(made, their_made, i) for i in (2, 3)]
    near_got.append(plane[1](near[1]))
    low_grad, first, second, made, their_made, *moved = tie(
        low_grad, first, second, made, their_made, *got[0], *got[1]
    )
    out_blocks = {
        2: shared(made, their_made, 2, moved[: sharing - 1]),
        3: shared(made, their_made, 3, moved[sharing - 1 :]),
    }

    third = line[1](second)
    got = to_share(made, their_made, 1)
    near_rows = jnp.concatenate([low_grad, first, second])
    others = to_core(near_rows)
    third, near_rows, others, near_got[1], near[2], *moved = tie(
        third, near_rows, others, near_got[1], near[2], *got
    )
    out_blocks[1] = shared(made, their_made, 1, moved)

    other_third = to_core(third)
    out_low = [out_blocks[i].astype(BF16) for i in range(1, LINES)]
    third, other_third, made, their_made, *out_low = tie(
        third, other_third, made, their_made, *out_low
    )

    out_got = [line[i](out_low[i - 1]) for i in range(1, LINES)]
    out_last = to_share(made, their_made, 0)
    near_got.append(plane[1](near[2]))
    branch, qkv_low, gain_parts, in_gain_part, mine, theirs = attention_backward(
        scalars,
        (near_rows, third, others, other_third),
        w_slots,
        w_out,
        gain_q,
        gain_k,
        cosine,
        sine,
        pre,
        q,
        k,
        v,
        attended,
        inverse,
        row_parts,
    )
    branch, qkv_low, gain_parts, in_gain_part, mine, theirs, near_got[2], made, *out_got = tie(
        branch, qkv_low, gain_parts, in_gain_part, mine, theirs, near_got[2], made, *out_got, *out_last
    )
    out_got, out_last = out_got[: LINES - 1], out_got[LINES - 1 :]

    theirs = to_core(theirs)
    small_part = jnp.concatenate(
        [from_slots(in_gain_part[:1]), jnp.sum(mid_gain_part, axis=0)[None], router_part]
    )
    small_part = small_part.reshape(experts + 2, groups, piece).transpose(1, 0, 2)
    gain_parts = jnp.concatenate(
        [gain_parts[0].reshape(groups, part), gain_parts[1].reshape(groups, part)], axis=1
    )
    gain_parts = jnp.pad(gain_parts, ((0, 0), (0, piece - 2 * part)))[:, None]
    small_part = jnp.concatenate([small_part, gain_parts], axis=1)
    small_part = small_part.reshape(LINES, columns, experts + 3, piece)
    small_part = xor_order(xor_order(small_part, 0, tz), 1, gc)
    small_part = small_part + to_core(small_part)
    w_part = dot_rows(a1, qkv_low).astype(BF16).reshape(columns, LINES * piece, -1)
    near_got = jnp.concatenate(near_got)
    mine, theirs, w_part, small_part, near_got, attended, branch = tie(
        mine, theirs, w_part, small_part, near_got, attended, branch
    )

    def both(i):
        return at_line(mine, i).astype(F32) + at_line(theirs, i).astype(F32)

    def start_scatter(held, bit):
        leaving = sorted(s for s in held if s & bit)
        return plane[bit](jnp.stack([held[s].astype(BF16) for s in leaving]))

    def end_scatter(held, bit, got):
        leaving = sorted(s for s in held if s & bit)
        return {
            s: v.astype(F32) + got[leaving.index(s ^ bit)].astype(F32)
            for s, v in held.items()
            if not s & bit
        }

    def two_ways(blocks):
        middle = blocks.shape[2] // 2
        halves = blocks[..., :middle], blocks[..., middle:]
        return [(dict(enumerate(half)), bits) for half, bits in zip(halves, (axes[::-1], axes))]

    def start_ways(ways, n):
        return [start_scatter(held, bits[n]) for held, bits in ways]

    def end_ways(ways, n, got):
        return [(end_scatter(held, bits[n], v), bits) for (held, bits), v in zip(ways, got)]

    def rest_of_ways(ways):
        for n in range(1, len(axes)):
            ways = end_ways(ways, n, start_ways(ways, n))
        return [held[0] for held, _ in ways]

    first = line[1](both(1).astype(BF16))
    third = line[1](both(3).astype(BF16))
    w_ways = two_ways(w_part)
    w_got = start_ways(w_ways, 0)
    small_got = line[2](small_part[2:])
    out_parts = dot_rows(attended, branch).reshape(local_heads, head, width)
    expert_sum = over_replicas(own + near_got.astype(F32)).astype(BF16)
    mine, theirs, first, third, out_parts, expert_sum, small_got, small_part, *w_got = tie(
        mine, theirs, first, third, out_parts, expert_sum, small_got, small_part, *w_got
    )
    small_part = small_part[:2] + small_got
    w_ways = end_ways(w_ways, 0, w_got)

    second = line[2]((both(2) + third.astype(F32)).astype(BF16))
    w_parts = rest_of_ways(w_ways)
    expert_other = to_core(expert_sum)
    small_got = line[1](small_part[1])
    layer_out = mid + shared(made, their_made, 0, out_last) + sum(v.astype(F32) for v in out_got)
    layer_out = layer_out.astype(BF16)
    second, expert_other, expert_sum, layer_out, out_parts, small_part, small_got, *w_parts = tie(
        second, expert_other, expert_sum, layer_out, out_parts, small_part, small_got, *w_parts
    )
    small_part = small_part[0] + small_got

    w_part = over_replicas(jnp.concatenate(w_parts, axis=1))
    rel = xor_order(w_part.reshape(LINES, piece, -1), 0, tz)
    rel_low = rel.astype(BF16)
    rel_got = [line[i](rel_low[i]) for i in range(1, LINES)]
    if out_heads == 1:
        zeros = jnp.zeros_like(out_parts)
        out_parts = jnp.where(
            swapped, jnp.stack([zeros, out_parts], 1), jnp.stack([out_parts, zeros], 1)
        ).reshape(columns, head, width)
    out_ways = two_ways(out_parts)
    out_more = start_ways(out_ways, 0)
    normed_grad = from_slots(both(0) + first.astype(F32) + second.astype(F32))
    in_back, _ = norm_back(normed_grad, inputs, row_scale(inputs), gain_in)
    input_grad = (mid_grad + in_back).astype(BF16)
    leaving = jnp.concatenate([layer_out, input_grad], axis=1)
    rel_own, leaving, small_part, *moved = tie(rel[0], leaving, small_part, *rel_got, *out_more)
    rel_got, out_more = moved[: LINES - 1], moved[LINES - 1 :]
    out_ways = end_ways(out_ways, 0, out_more)

    going = send_home(leaving)
    for bit in axes[::-1]:
        small_part = small_part[:bit] + plane[bit](small_part[bit : 2 * bit])
    small_part = small_part[0]
    small_part = small_part + sum(move(small_part) for move in mv["replicas"])
    out_own = over_replicas(jnp.concatenate(rest_of_ways(out_ways), axis=1))
    own_cols = xor_order(jnp.stack([rel_own] + [v.astype(F32) for v in rel_got]), 0, tz)
    other_cols = to_core(own_cols)
    core_scalar = core.reshape(1).astype(jnp.int32)
    gate_total, up_total, down_total = join_expert_grads(core_scalar, expert_sum, expert_other)
    out_own, own_cols, other_cols, gate_total, up_total, down_total, small_part, *going = tie(
        out_own, own_cols, other_cols, gate_total, up_total, down_total, small_part, *going
    )

    out_other = to_core(out_own)
    out_total = whole(out_own, out_other, 0) if out_heads == 2 else out_own + out_other
    query_total, key_total, value_total = join_column_grads(core_scalar, own_cols, other_cols, head)
    arrived = at_home(going)

    return (
        arrived[..., :width],
        arrived[..., width:].astype(F32),
        small_part[0],
        query_total,
        key_total,
        value_total,
        small_part[experts + 2, :part],
        small_part[experts + 2, part : 2 * part],
        out_total,
        small_part[1],
        small_part[2 : experts + 2].T,
        gate_total[None],
        up_total[None],
        down_total[None],
    )


def solution(mesh):
    tokens = P("rep", None, "grp", None)
    rows = P("grp", None)
    vector = P("grp")
    stacked = P("grp", None, None)
    return jax.shard_map(
        per_device,
        mesh=mesh,
        in_specs=(
            tokens,
            tokens,
            tokens,
            vector,
            rows,
            rows,
            rows,
            vector,
            vector,
            rows,
            vector,
            rows,
            stacked,
            stacked,
            stacked,
        ),
        out_specs=(
            tokens,
            tokens,
            vector,
            rows,
            rows,
            rows,
            vector,
            vector,
            rows,
            vector,
            rows,
            stacked,
            stacked,
            stacked,
        ),
        check_vma=False,
    )
```
